256 devices in a mesh: dst: 32 (over x, z), src: 8 (over y, core).
Axes of the slice: x: 4, y: 4, z: 8, core: 2. Of those that a mesh axis runs over, the one named last changes fastest.
Arguments:
- node_feats: bfloat16 [8, 32, 256, 128], P('src', 'dst'), may hold values from -16 to 16
- w_query: bfloat16 [128, 128], replicated, may hold values from -1 to 1
- w_key: bfloat16 [128, 128], replicated, may hold values from -1 to 1
- w_value: bfloat16 [128, 128], replicated, may hold values from -0.5 to 0.5
- w_out: bfloat16 [128, 128], replicated, may hold values from -0.5 to 0.5
- src_blocks: int32 [8, 32, 16, 16], P('src', 'dst'), may hold values from 0 to 63, as said below
- live_counts: int32 [8, 32, 16], P('src', 'dst'), may hold values from 1 to 16, as said below
- edge_bits: int32 [8, 32, 16, 16, 16, 128], P('src', 'dst'), may hold values from 0 to 255, as said below
Outputs:
- mixed_rows: bfloat16 [8, 32, 256, 128], P('src', 'dst')
The draws below stay inside these ranges and needn't reach their ends.
Inputs may be any that keep to these rules, and one draw needn't show every extreme that they name: `src_blocks`: each list holds 16 different source block numbers of its source group. Entries from live_counts onward in a list are unused; 16 is reached in every draw. `edge_bits`: in list entry 0 every row t links to column t.
All inputs are finite; a program needn't handle non-finite values.
Results may differ from the reference program's by a relative error of at most 0.015.
Values may be sent and summed in bfloat16 or wider, within the bound.
No kernel may reach another device: no remote copies, remote signals or barrier semaphores. Data moves between devices by JAX's collectives and lax.ppermute only.
A program may use at most 64 MiB of HBM per device.

```python
import math
import jax
import jax.numpy as jnp
from jax import lax

D = 128
HEADS = 4
BLK = 128
SLOTS = 16
ROWS = 256
DBLK = 16
SBLK = 64
WORDS = 16
N_DST = 32
N_SRC = 8


def draw_node_feats(key, part):
    key = jax.random.fold_in(key, 11)
    noise_key = jax.random.fold_in(key, 0)
    shape = (N_SRC, N_DST, ROWS, D)
    return jnp.clip(jax.random.normal(noise_key, shape, jnp.float32), -6.0, 6.0).astype(jnp.bfloat16)


def draw_src_blocks(key, part):
    key = jax.random.fold_in(key, 23)
    list_total = N_SRC * N_DST * DBLK
    list_keys = jax.random.split(key, list_total)
    lists_drawn = jax.vmap(lambda one_key: jax.random.permutation(one_key, SBLK)[:SLOTS])(list_keys)
    return lists_drawn.reshape(N_SRC, N_DST, DBLK, SLOTS).astype(jnp.int32)


def draw_live_counts(key, part):
    key = jax.random.fold_in(key, 37)
    level_key, drop_key, spot_key = jax.random.split(key, 3)
    drawn_level = jax.random.randint(level_key, (N_SRC, N_DST, 1), 1, SLOTS + 1)
    level = jnp.maximum(1, drawn_level * drawn_level // SLOTS)
    counts = level - jax.random.randint(drop_key, (N_SRC, N_DST, DBLK), 0, level // 2 + 1)
    flat_counts = counts.reshape(-1)
    spot = jax.random.randint(spot_key, (), 0, flat_counts.shape[0])
    flat_counts = jnp.where(jnp.arange(flat_counts.shape[0]) == spot, SLOTS, flat_counts)
    return flat_counts.reshape(N_SRC, N_DST, DBLK).astype(jnp.int32)


def draw_edge_bits(key, part):
    key = jax.random.fold_in(key, 41)
    first_key, second_key = jax.random.split(key, 2)
    shape = (N_SRC, N_DST, DBLK, SLOTS, WORDS, BLK)
    packed = jnp.bitwise_and(jax.random.randint(first_key, shape, 0, 256), jax.random.randint(second_key, shape, 0, 256))
    row_ids = jnp.arange(BLK, dtype=jnp.int32)
    word_ids = jnp.arange(WORDS, dtype=jnp.int32)
    own_bit = jnp.left_shift(jnp.ones((BLK,), jnp.int32), row_ids % 8)
    own_words = jnp.where(word_ids[:, None] == (row_ids // 8)[None, :], own_bit[None, :], 0).astype(jnp.int32)
    first_slot = jnp.arange(SLOTS, dtype=jnp.int32) == 0
    extra = jnp.where(first_slot[:, None, None], own_words[None], 0).astype(jnp.int32)
    return jnp.bitwise_or(packed, extra).astype(jnp.int32)


def scatter_about(own_key, extent, width, bound, kind=jnp.bfloat16):
    return jnp.clip(width * jax.random.normal(own_key, extent, jnp.float32), -bound, bound).astype(kind)


def setup_inputs(seed: int = 0) -> dict:
    keys = jax.random.split(jax.random.key(seed), 9)
    return {
        "node_feats": draw_node_feats(jax.random.fold_in(keys[8], 71), 0),
        "w_query": scatter_about(keys[1], (D, D), (D // 3) ** -0.5, 1.0),
        "w_key": scatter_about(keys[2], (D, D), (D // 3) ** -0.5, 1.0),
        "w_value": scatter_about(keys[3], (D, D), D ** -0.5, 0.5),
        "w_out": scatter_about(keys[4], (D, D), D ** -0.5, 0.5),
        "src_blocks": draw_src_blocks(jax.random.fold_in(keys[8], 71), 0),
        "live_counts": draw_live_counts(jax.random.fold_in(keys[8], 71), 0),
        "edge_bits": draw_edge_bits(jax.random.fold_in(keys[8], 71), 0),
    }


def project_rows(flat_rows, weight):
    return jnp.dot(flat_rows, weight, preferred_element_type=jnp.float32).astype(jnp.bfloat16)

def reference(node_feats, w_query, w_key, w_value, w_out, src_blocks, live_counts, edge_bits):
    group_src, group_dst, row_count, model_width = node_feats.shape
    head_dim = model_width // HEADS
    per_group = row_count // BLK
    flat_rows = node_feats.reshape(-1, model_width)
    queries = project_rows(flat_rows, w_query).reshape(group_src, group_dst, per_group, BLK, HEADS, head_dim)
    key_rows = project_rows(flat_rows, w_key).reshape(group_src, group_dst * per_group, BLK, HEADS, head_dim)
    value_rows = project_rows(flat_rows, w_value).reshape(group_src, group_dst * per_group, BLK, HEADS, head_dim)
    query_blocks = jnp.transpose(queries, (1, 0, 2, 3, 4, 5)).reshape(-1, BLK, HEADS, head_dim)
    lists_all = jnp.transpose(src_blocks, (1, 2, 0, 3)).reshape(-1, group_src, SLOTS)
    counts_all = jnp.transpose(live_counts, (1, 2, 0)).reshape(-1, group_src)
    words_all = jnp.transpose(edge_bits, (1, 2, 0, 3, 4, 5)).reshape(-1, group_src, SLOTS, WORDS, BLK)
    group_ids = jnp.arange(group_src, dtype=jnp.int32)[:, None]
    slot_ids = jnp.arange(SLOTS, dtype=jnp.int32)
    bit_shifts = jnp.arange(8, dtype=jnp.int32)
    scale_factor = 1.0 / math.sqrt(head_dim)

    def one_block(block_args):
        query_block, block_lists, block_counts, block_words = block_args
        keys_here = key_rows[group_ids, block_lists].astype(jnp.float32)
        values_here = value_rows[group_ids, block_lists].astype(jnp.float32)
        scores = jnp.einsum('jschd,thd->hjsct', keys_here, query_block.astype(jnp.float32)) * scale_factor
        bit_values = jnp.bitwise_and(jnp.right_shift(block_words[:, :, :, None, :], bit_shifts[:, None]), 1)
        linked = bit_values.reshape(group_src, SLOTS, BLK, BLK) == 1
        linked = linked & (slot_ids[None, :] < block_counts[:, None])[:, :, None, None]
        group_peak = lax.optimization_barrier(jnp.max(jnp.where(linked[None], scores, -jnp.inf), axis=(2, 3)))
        weights = jnp.where(linked[None], jnp.exp(scores - group_peak[:, :, None, None, :]), 0.0)
        group_sum = lax.optimization_barrier(jnp.sum(weights, axis=(2, 3)))
        rounded = lax.optimization_barrier(weights.astype(jnp.bfloat16)).astype(jnp.float32)
        group_acc = jnp.einsum('hjsct,jschd->jthd', rounded, values_here)
        group_out = (group_acc / jnp.transpose(group_sum, (1, 2, 0))[..., None]).astype(jnp.bfloat16)
        group_out = lax.optimization_barrier(group_out).astype(jnp.float32)
        row_peak = lax.optimization_barrier(jnp.max(group_peak, axis=1))
        mass = group_sum * jnp.exp(group_peak - row_peak[:, None, :])
        denominator = lax.optimization_barrier(jnp.sum(mass, axis=1))
        numerator = jnp.einsum('hjt,jthd->thd', mass, group_out)
        return (numerator / jnp.transpose(denominator)[:, :, None]).reshape(BLK, model_width).astype(jnp.bfloat16)
    attended = lax.map(one_block, (query_blocks, lists_all, counts_all, words_all))
    mixed_rows = jnp.dot(attended.reshape(-1, model_width), w_out, preferred_element_type=jnp.float32).astype(jnp.bfloat16)
    mixed_rows = mixed_rows.reshape(group_dst, group_src, row_count, model_width)
    return jnp.transpose(mixed_rows, (1, 0, 2, 3))
```

```python
import functools
import math

import jax
import jax.numpy as jnp
from jax import lax
from jax.experimental import pallas as pl
from jax.experimental.pallas import tpu as pltpu
from jax.sharding import PartitionSpec as P

HEADS = 4
BLK = 128
HEAD = 32
DESTS = 16
SLOTS = 16
ITEMS = 136
NEG = -1e30
MSG = 160
BF16 = jnp.bfloat16
F32 = jnp.float32
NT = (((1,), (1,)), ((), ()))
TN = (((0,), (0,)), ((), ()))


def vmem():
    return pl.BlockSpec(memory_space=pltpu.VMEM)


def smem():
    return pl.BlockSpec(memory_space=pltpu.SMEM)


def prep_kernel(rows_ref, wqt_ref, qbd_ref):
    scale = math.log2(math.e) / math.sqrt(HEAD)
    qbd_ref[...] = jnp.zeros_like(qbd_ref)

    def body(i, carry):
        rows = rows_ref[i]
        qt = lax.dot_general(wqt_ref[...], rows, NT, preferred_element_type=F32)
        qs = qt.astype(BF16).astype(F32) * scale
        high = qs.astype(BF16)
        low = (qs - high.astype(F32)).astype(BF16)
        for k in range(2):
            for h in range(HEADS):
                r = slice(h * HEAD, (h + 1) * HEAD)
                c = slice(h * BLK, (h + 1) * BLK)
                t = slice(k * BLK, (k + 1) * BLK)
                qbd_ref[2 * i + k, r, c] = high[r, t]
                qbd_ref[2 * i + k, BLK + h * HEAD : BLK + (h + 1) * HEAD, c] = low[r, t]
        return carry

    lax.fori_loop(0, DESTS // 2, body, 0)


def project(chunk_refs, wk_ref, wvt_ref, k_ref, vt_ref):
    for n, chunk_ref in enumerate(chunk_refs):
        per = chunk_ref.shape[0] // 256

        def body(i, carry, n=n, chunk_ref=chunk_ref, per=per):
            rows = chunk_ref[pl.ds(i * 256, 256), :]
            keys = jnp.dot(rows, wk_ref[...], preferred_element_type=F32).astype(BF16)
            vals = lax.dot_general(wvt_ref[...], rows, NT, preferred_element_type=F32).astype(BF16)
            at = (n * per + i) * 2
            for k in range(2):
                t = slice(k * BLK, (k + 1) * BLK)
                k_ref[at + k] = keys[t]
                vt_ref[at + k] = vals[:, t]
            return carry

        lax.fori_loop(0, per, body, 0)


def visit(items_ref, count, words_ref, qbd_ref, k_ref, vt_ref, m_ref, l_ref, acc_ref, s_ref, x_ref, w_ref, f_ref):
    sub_iota = lax.broadcasted_iota(jnp.int32, (8, BLK), 0)
    bit = jnp.left_shift(jnp.ones((8, BLK), jnp.int32), sub_iota)
    ones = jnp.ones((16, 2 * BLK), BF16)

    def fields(i):
        p1 = items_ref[0, i]
        p2 = items_ref[1, i]
        live1 = lax.shift_right_logical(p1, 16)
        live2 = lax.shift_right_logical(p2, 16)
        w1 = p1 & 255
        w2 = p2 & 255
        b1 = lax.shift_right_logical(p1, 8) & 255
        b2 = lax.shift_right_logical(p2, 8) & 255
        q = lax.shift_right_logical(w1, 4)
        return q, jnp.where(live1 == 1, q, DESTS), b1, b2, w1, w2, live1, live2

    def body(i, carry):
        _, qd, b1, b2, _, _, _, _ = fields(i)
        for p in range(2):
            r = slice(64 * p, 64 * p + 64)
            lhs = jnp.concatenate([vt_ref[b1, r, :], vt_ref[b2, r, :]], axis=1)
            lhs = jnp.concatenate([lhs, ones], axis=0)
            o = jnp.dot(lhs, w_ref[:, 256 * p : 256 * p + 256], preferred_element_type=F32)
            for k in range(2):
                h = 2 * p + k
                c = slice(BLK * k, BLK * k + BLK)
                fac = f_ref[h : h + 1, :]
                a = slice(h * HEAD, (h + 1) * HEAD)
                acc_ref[qd, a, :] = acc_ref[qd, a, :] * fac + o[k * HEAD : (k + 1) * HEAD, c]
                l_ref[qd, h : h + 1, :] = l_ref[qd, h : h + 1, :] * fac + o[64:65, c]
        _, qd, _, _, _, _, _, _ = fields(i + 1)
        for h in range(HEADS):
            c = slice(BLK * h, BLK * h + BLK)
            old = m_ref[qd, h : h + 1, :]
            new = jnp.maximum(old, x_ref[h : h + 1, :])
            f_ref[h : h + 1, :] = jnp.exp2(old - new)
            m_ref[qd, h : h + 1, :] = new
            w_ref[:, c] = jnp.exp2(s_ref[:, c] - new).astype(BF16)
        q, _, b1, b2, w1, w2, live1, live2 = fields(i + 2)
        kk = jnp.concatenate([k_ref[b1], k_ref[b2]], axis=0)
        lhs = jnp.concatenate([kk, kk], axis=1)
        words = [words_ref[w1] * live1, words_ref[w2] * live2]
        for p in range(2):
            s = jnp.dot(lhs, qbd_ref[q, :, 256 * p : 256 * p + 256], preferred_element_type=F32)
            peak = [None, None]
            for g in range(32):
                row = words[g // 16][g % 16 : g % 16 + 1, :]
                hit = (jnp.broadcast_to(row, (8, BLK)) & bit) != 0
                for k in range(2):
                    v = jnp.where(hit, s[8 * g : 8 * g + 8, BLK * k : BLK * k + BLK], NEG)
                    s_ref[8 * g : 8 * g + 8, 256 * p + BLK * k : 256 * p + BLK * k + BLK] = v
                    peak[k] = v if peak[k] is None else jnp.maximum(peak[k], v)
            for k in range(2):
                x_ref[2 * p + k : 2 * p + k + 1, :] = jnp.max(peak[k], axis=0, keepdims=True)
        return carry

    lax.fori_loop(0, count + 2, body, 0)


def phase_kernel(first, last, n_chunks, items_ref, count_ref, words_ref, qbd_ref, wk_ref, wvt_ref, *refs):
    chunks = refs[:n_chunks]
    refs = refs[n_chunks:]
    if first:
        state_in = None
    else:
        state_in, refs = refs[:3], refs[3:]
    if last:
        msg_ref, refs = refs[0], refs[1:]
    else:
        state_out, refs = refs[:3], refs[3:]
    k_ref, vt_ref, m_ref, l_ref, acc_ref, s_ref, x_ref, w_ref, f_ref = refs
    project(chunks, wk_ref, wvt_ref, k_ref, vt_ref)
    if first:
        m_ref[...] = jnp.full_like(m_ref, NEG)
        l_ref[...] = jnp.zeros_like(l_ref)
        acc_ref[...] = jnp.zeros_like(acc_ref)
    else:
        m_ref[:DESTS] = state_in[0][...]
        l_ref[:DESTS] = state_in[1][...]
        acc_ref[:DESTS] = state_in[2][...]
        m_ref[DESTS] = jnp.full((8, BLK), NEG, F32)
    s_ref[...] = jnp.zeros_like(s_ref)
    w_ref[...] = jnp.zeros_like(w_ref)
    x_ref[...] = jnp.zeros_like(x_ref)
    f_ref[...] = jnp.zeros_like(f_ref)
    visit(items_ref, count_ref[0], words_ref, qbd_ref, k_ref, vt_ref, m_ref, l_ref, acc_ref, s_ref, x_ref, w_ref, f_ref)
    if last:
        def emit(q, carry):
            top = m_ref[q, :HEADS, :]
            tot = l_ref[q, :HEADS, :]
            for h in range(HEADS):
                a = slice(h * HEAD, (h + 1) * HEAD)
                msg_ref[q, a, :] = (acc_ref[q, a, :] / tot[h : h + 1, :]).astype(BF16)
            parts = []
            for v in (top, tot):
                for _ in range(3):
                    piece = v.astype(BF16).astype(F32)
                    parts.append(piece)
                    v = v - piece
            parts.append(jnp.zeros((8, BLK), F32))
            msg_ref[q, BLK:, :] = jnp.concatenate(parts, axis=0).astype(BF16)
            return carry

        lax.fori_loop(0, DESTS, emit, 0)
    else:
        state_out[0][...] = m_ref[:DESTS]
        state_out[1][...] = l_ref[:DESTS]
        state_out[2][...] = acc_ref[:DESTS]


def run_phase(first, last, items, count, words, qbd, wk, wvt, chunks, state):
    blocks = sum(c.shape[0] for c in chunks) // BLK
    state_shape = (
        jax.ShapeDtypeStruct((DESTS, 8, BLK), F32),
        jax.ShapeDtypeStruct((DESTS, 8, BLK), F32),
        jax.ShapeDtypeStruct((DESTS, BLK, BLK), F32),
    )
    out_shape = jax.ShapeDtypeStruct((DESTS, MSG, BLK), BF16) if last else state_shape
    n_in = 6 + len(chunks) + (0 if first else 3)
    return pl.pallas_call(
        functools.partial(phase_kernel, first, last, len(chunks)),
        out_shape=out_shape,
        in_specs=[smem(), smem()] + [vmem()] * (n_in - 2),
        out_specs=vmem() if last else (vmem(),) * 3,
        scratch_shapes=[
            pltpu.VMEM((blocks, BLK, BLK), BF16),
            pltpu.VMEM((blocks, BLK, BLK), BF16),
            pltpu.VMEM((DESTS + 1, 8, BLK), F32),
            pltpu.VMEM((DESTS + 1, 8, BLK), F32),
            pltpu.VMEM((DESTS + 1, BLK, BLK), F32),
            pltpu.VMEM((2 * BLK, HEADS * BLK), F32),
            pltpu.VMEM((8, BLK), F32),
            pltpu.VMEM((2 * BLK, HEADS * BLK), BF16),
            pltpu.VMEM((8, BLK), F32),
        ],
        compiler_params=pltpu.CompilerParams(vmem_limit_bytes=40 * 1024 * 1024),
        cost_estimate=pl.CostEstimate(flops=500_000_000, bytes_accessed=8_000_000, transcendentals=4_000_000),
    )(items, count, words, qbd, wk, wvt, *chunks, *(() if first else state))


def combine_kernel(msg_ref, wo_ref, out_ref):
    sources = msg_ref.shape[0]
    for b in range(2):
        stats = []
        for j in range(sources):
            st = msg_ref[j, b, BLK:, :].astype(F32)
            stats.append((st[0:4] + st[4:8] + st[8:12], st[12:16] + st[16:20] + st[20:24]))
        peak = functools.reduce(jnp.maximum, [s[0] for s in stats])
        mass = [tot * jnp.exp2(top - peak) for top, tot in stats]
        denom = functools.reduce(jnp.add, mass)
        rows = []
        for h in range(HEADS):
            a = slice(h * HEAD, (h + 1) * HEAD)
            num = functools.reduce(
                jnp.add,
                [msg_ref[j, b, a, :].astype(F32) * mass[j][h : h + 1, :] for j in range(sources)],
            )
            rows.append(num / denom[h : h + 1, :])
        att = jnp.concatenate(rows, axis=0).astype(BF16)
        mixed = lax.dot_general(att, wo_ref[...], TN, preferred_element_type=F32)
        out_ref[b * BLK : (b + 1) * BLK, :] = mixed.astype(BF16)


def make_items(lists, counts, my_dst):
    my_x, my_z = my_dst // 8, my_dst % 8
    owner = lists // 2
    dx = (owner // 8 - my_x) % 4
    dz = (owner % 8 - my_z) % 8
    at_z = 2 * jnp.minimum(dz, 8 - dz) - (dz >= 4).astype(jnp.int32)
    chunk = jnp.where(dx == 1, 1, 0)
    pos = (chunk * 8 + at_z) * 2 + lists % 2
    phase = jnp.where(dx == 0, 0, jnp.where(dx == 2, 2, 1))
    slots = jnp.arange(SLOTS, dtype=jnp.int32)
    dests = jnp.arange(DESTS, dtype=jnp.int32)
    word = dests[:, None] * SLOTS + slots[None, :]
    live = slots[None, :] < counts[:, None]
    pay = word | (pos << 8) | (1 << 16)
    sel = live[None] & (phase[None] == jnp.arange(3, dtype=jnp.int32)[:, None, None])
    sel_i = sel.astype(jnp.int32)
    before = (slots[None, :] < slots[:, None]).astype(jnp.int32)
    rank = jnp.sum(sel_i[:, :, None, :] * before[None, None], axis=-1)
    per_dest = (jnp.sum(sel_i, axis=-1) + 1) // 2
    offset = jnp.sum(per_dest[:, None, :] * before[None], axis=-1)
    total = jnp.sum(per_dest, axis=-1)
    item = jnp.where(sel, offset[:, :, None] + rank // 2 + 2, -1)
    key = (item * 2 + rank % 2).reshape(3, 1, DESTS * SLOTS)
    want = jnp.arange(2 * ITEMS, dtype=jnp.int32)
    want = (want % ITEMS) * 2 + want // ITEMS
    table = jnp.sum(jnp.where(key == want[None, :, None], pay.reshape(1, 1, -1), 0), axis=-1)
    return table.reshape(3, 2, ITEMS), total


def z_step(rows, step):
    return lax.ppermute(rows, "dst", [(x * 8 + z, x * 8 + (z + step) % 8) for x in range(4) for z in range(8)])


def x_step(rows, step):
    return lax.ppermute(rows, "dst", [(x * 8 + z, ((x + step) % 4) * 8 + z) for x in range(4) for z in range(8)])


def shards(node_feats, w_query, w_key, w_value, w_out, src_blocks, live_counts, edge_bits):
    own = node_feats[0, 0]
    near = [own] + [z_step(own, s) for s in (1, -1, 2, -2, 3, -3, 4)]
    base = jnp.concatenate(near, axis=0)
    left = x_step(base, 1)
    right = x_step(base, -1)
    far = x_step(base, 2)
    dest_rows = lax.all_gather(own, "src", axis=0, tiled=False)
    items, total = make_items(src_blocks[0, 0], live_counts[0, 0], lax.axis_index("dst"))
    words = edge_bits[0, 0].reshape(DESTS * SLOTS, 16, BLK)
    qbd = pl.pallas_call(
        prep_kernel,
        out_shape=jax.ShapeDtypeStruct((DESTS, 2 * BLK, HEADS * BLK), BF16),
        in_specs=[vmem(), vmem()],
        out_specs=vmem(),
    )(dest_rows, w_query.T)
    wvt = w_value.T
    run = functools.partial(run_phase, words=words, qbd=qbd, wk=w_key, wvt=wvt)
    state = run(True, False, items[0], total[0:1], chunks=[base], state=None)
    state = run(False, False, items[1], total[1:2], chunks=[left, right], state=state)
    msg = run(False, True, items[2], total[2:3], chunks=[far], state=state)
    got = lax.all_to_all(msg.reshape(8, 2, MSG, BLK), "src", 0, 0, tiled=True)
    mixed = pl.pallas_call(
        combine_kernel,
        out_shape=jax.ShapeDtypeStruct((2 * BLK, BLK), BF16),
        in_specs=[vmem(), vmem()],
        out_specs=vmem(),
    )(got, w_out)
    return mixed.reshape(1, 1, 2 * BLK, BLK)


def solution(mesh):
    in_specs = (
        P("src", "dst", None, None),
        P(),
        P(),
        P(),
        P(),
        P("src", "dst", None, None),
        P("src", "dst", None),
        P("src", "dst", None, None, None, None),
    )
    out_specs = P("src", "dst", None, None)
    return jax.shard_map(shards, mesh=mesh, in_specs=in_specs, out_specs=out_specs, check_vma=False)
```

```python
import functools
import math

import jax
import jax.numpy as jnp
from jax import lax
from jax.experimental import pallas as pl
from jax.experimental.pallas import tpu as pltpu
from jax.sharding import PartitionSpec as P

HEADS = 4
BLK = 128
HEAD = 32
DESTS = 16
SLOTS = 16
ITEMS = 144
NEG = -1e30
MSG = 144
LIMIT = 100.0
SCALE = math.log2(math.e) / math.sqrt(HEAD)
BF16 = jnp.bfloat16
F32 = jnp.float32
NT = (((1,), (1,)), ((), ()))
TN = (((0,), (0,)), ((), ()))


def vmem():
    return pl.BlockSpec(memory_space=pltpu.VMEM)


def smem():
    return pl.BlockSpec(memory_space=pltpu.SMEM)


def copy_kernel(own_ref, out_ref):
    for i in range(8):
        out_ref[i] = own_ref[...]


def prep_kernel(me_ref, *refs):
    row_refs, (wq_ref, wv_ref, qbd_ref, wvt_ref, qnorm_ref) = refs[:8], refs[8:]
    qbd_ref[...] = jnp.zeros_like(qbd_ref)
    wvt_ref[...] = wv_ref[...].T
    wqt = wq_ref[...].T
    norm = jnp.zeros((HEADS, 2 * BLK), F32)
    for step in range(8):
        owner = (me_ref[0] - step) & 7
        qt = lax.dot_general(wqt, row_refs[step][...], NT, preferred_element_type=F32).astype(BF16)
        wide = qt.astype(F32)
        norm = jnp.maximum(norm, jnp.sum((wide * wide).reshape(HEADS, HEAD, 2 * BLK), axis=1))
        for k in range(2):
            for h in range(HEADS):
                r = slice(h * HEAD, (h + 1) * HEAD)
                qbd_ref[2 * owner + k, r, h * BLK : (h + 1) * BLK] = qt[r, k * BLK : (k + 1) * BLK]
    qnorm_ref[...] = norm


def project(chunk_refs, wk_ref, wvt_ref, k_ref, vt_ref, norm_ref):
    col = lax.shift_right_logical(lax.broadcasted_iota(jnp.int32, (BLK, BLK), 0), 5)
    row = lax.shift_right_logical(lax.broadcasted_iota(jnp.int32, (BLK, BLK), 1), 5)
    same = (col == row).astype(BF16)
    norm_ref[...] = jnp.zeros_like(norm_ref)
    for n, chunk_ref in enumerate(chunk_refs):
        per = chunk_ref.shape[0] // 512

        def body(i, carry, n=n, chunk_ref=chunk_ref, per=per):
            rows = chunk_ref[pl.ds(i * 512, 512), :]
            keys = jnp.dot(rows, wk_ref[...], preferred_element_type=F32).astype(BF16)
            vals = lax.dot_general(wvt_ref[...], rows, NT, preferred_element_type=F32).astype(BF16)
            wide = keys.astype(F32)
            norms = jnp.dot((wide * wide).astype(BF16), same, preferred_element_type=F32)
            norm_ref[...] = jnp.maximum(norm_ref[...], jnp.max(norms.reshape(64, 8, BLK), axis=0))
            at = (n * per + i) * 4
            for k in range(4):
                t = slice(k * BLK, (k + 1) * BLK)
                k_ref[at + k] = keys[t]
                vt_ref[at + k] = vals[:, t]
            return carry

        lax.fori_loop(0, per, body, 0, unroll=4)


def fields(items_ref, i):
    p1 = items_ref[0, i]
    p2 = items_ref[1, i]
    live1 = lax.shift_right_logical(p1, 16)
    live2 = lax.shift_right_logical(p2, 16)
    w1 = p1 & 255
    w2 = p2 & 255
    b1 = lax.shift_right_logical(p1, 8) & 255
    b2 = lax.shift_right_logical(p2, 8) & 255
    q = lax.shift_right_logical(w1, 4)
    return q, jnp.where(live1 == 1, q, DESTS), b1, b2, w1, w2, live1, live2


def bit_of_row():
    sub_iota = lax.broadcasted_iota(jnp.int32, (8, BLK), 0)
    return jnp.left_shift(jnp.ones((8, BLK), jnp.int32), sub_iota)


def visit_bounded(items_ref, count, words_ref, qbd_ref, k_ref, vt_ref, l_ref, acc_ref, w_refs):
    bit = bit_of_row()
    ones = jnp.ones((16, 2 * BLK), BF16)

    def gather_values(i, w_ref):
        _, qd, b1, b2, _, _, _, _ = fields(items_ref, i)
        for p in range(2):
            r = slice(64 * p, 64 * p + 64)
            lhs = jnp.concatenate([vt_ref[b1, r, :], vt_ref[b2, r, :]], axis=1)
            lhs = jnp.concatenate([lhs, ones], axis=0)
            o = jnp.dot(lhs, w_ref[:, 256 * p : 256 * p + 256], preferred_element_type=F32)
            for k in range(2):
                h = 2 * p + k
                c = slice(BLK * k, BLK * k + BLK)
                a = slice(h * HEAD, (h + 1) * HEAD)
                acc_ref[qd, a, :] += o[k * HEAD : (k + 1) * HEAD, c]
                l_ref[qd, h : h + 1, :] += o[64:65, c]

    def weigh(i, w_ref):
        q, _, b1, b2, w1, w2, live1, live2 = fields(items_ref, i)
        kk = jnp.concatenate([k_ref[b1], k_ref[b2]], axis=0)
        words = [words_ref[w1] * live1, words_ref[w2] * live2]
        for p in range(2):
            s = jnp.dot(kk, qbd_ref[q, :, 256 * p : 256 * p + 256], preferred_element_type=F32)
            for g in range(16):
                hits = []
                for u in (2 * g, 2 * g + 1):
                    line = words[u // 16][u % 16 : u % 16 + 1, :]
                    hits.append((jnp.broadcast_to(line, (8, BLK)) & bit) != 0)
                for k in range(2):
                    v = [
                        jnp.exp2(jnp.where(hits[u], s[16 * g + 8 * u : 16 * g + 8 * u + 8, BLK * k : BLK * k + BLK] * SCALE, NEG))
                        for u in range(2)
                    ]
                    c = slice(256 * p + BLK * k, 256 * p + BLK * k + BLK)
                    w_ref[16 * g : 16 * g + 16, c] = jnp.concatenate(v, axis=0).astype(BF16)

    def body(j, carry):
        for e in range(4):
            i = 4 * j + e
            weigh(i + 2, w_refs[e % 2])
            gather_values(i + 1, w_refs[1 - e % 2])
        return carry

    lax.fori_loop(0, lax.shift_right_logical(count + 4, 2), body, 0)


def visit(items_ref, count, words_ref, qbd_ref, k_ref, vt_ref, m_ref, l_ref, acc_ref, s_refs, x_refs, w_refs, f_refs):
    bit = bit_of_row()
    ones = jnp.ones((16, 2 * BLK), BF16)

    def gather_values(i, w_ref, f_ref):
        _, qd, b1, b2, _, _, _, _ = fields(items_ref, i)
        for p in range(2):
            r = slice(64 * p, 64 * p + 64)
            lhs = jnp.concatenate([vt_ref[b1, r, :], vt_ref[b2, r, :]], axis=1)
            lhs = jnp.concatenate([lhs, ones], axis=0)
            o = jnp.dot(lhs, w_ref[:, 256 * p : 256 * p + 256], preferred_element_type=F32)
            for k in range(2):
                h = 2 * p + k
                c = slice(BLK * k, BLK * k + BLK)
                fac = f_ref[h : h + 1, :]
                a = slice(h * HEAD, (h + 1) * HEAD)
                acc_ref[qd, a, :] = acc_ref[qd, a, :] * fac + o[k * HEAD : (k + 1) * HEAD, c]
                l_ref[qd, h : h + 1, :] = l_ref[qd, h : h + 1, :] * fac + o[64:65, c]

    def weigh(i, s_ref, x_ref, w_ref, f_ref):
        _, qd, _, _, _, _, _, _ = fields(items_ref, i)
        for h in range(HEADS):
            c = slice(BLK * h, BLK * h + BLK)
            old = m_ref[qd, h : h + 1, :]
            new = jnp.maximum(old, x_ref[h : h + 1, :])
            f_ref[h : h + 1, :] = jnp.exp2(old - new)
            m_ref[qd, h : h + 1, :] = new
            w_ref[:, c] = jnp.exp2(s_ref[:, c] - new).astype(BF16)

    def score(i, s_ref, x_ref):
        q, _, b1, b2, w1, w2, live1, live2 = fields(items_ref, i)
        kk = jnp.concatenate([k_ref[b1], k_ref[b2]], axis=0)
        words = [words_ref[w1] * live1, words_ref[w2] * live2]
        for p in range(2):
            s = jnp.dot(kk, qbd_ref[q, :, 256 * p : 256 * p + 256], preferred_element_type=F32)
            peak = [None, None]
            for g in range(32):
                row = words[g // 16][g % 16 : g % 16 + 1, :]
                hit = (jnp.broadcast_to(row, (8, BLK)) & bit) != 0
                for k in range(2):
                    v = jnp.where(hit, s[8 * g : 8 * g + 8, BLK * k : BLK * k + BLK] * SCALE, NEG)
                    s_ref[8 * g : 8 * g + 8, 256 * p + BLK * k : 256 * p + BLK * k + BLK] = v
                    peak[k] = v if peak[k] is None else jnp.maximum(peak[k], v)
            for k in range(2):
                x_ref[2 * p + k : 2 * p + k + 1, :] = jnp.max(peak[k], axis=0, keepdims=True)

    def body(j, carry):
        for e in range(2):
            i = 2 * j + e
            score(i + 2, s_refs[e], x_refs[e])
            gather_values(i, w_refs[e], f_refs[e])
            weigh(i + 1, s_refs[1 - e], x_refs[1 - e], w_refs[1 - e], f_refs[1 - e])
        return carry

    lax.fori_loop(0, lax.shift_right_logical(count + 3, 1), body, 0)


def phase_kernel(phase, n_chunks, items_ref, count_ref, bounded_ref, words_ref, qbd_ref, qnorm_ref, wk_ref, wvt_ref, *refs):
    first, last = phase == 0, phase == 2
    chunks, refs = refs[:n_chunks], refs[n_chunks:]
    if not first:
        refs = refs[3:]
    m_ref, l_ref, acc_ref, out_ref = refs[:4]
    k_ref, vt_ref, norm_ref = refs[4:7]
    s_refs, x_refs, w_refs, f_refs = refs[7:9], refs[9:11], refs[11:13], refs[13:15]
    items_ref = items_ref.at[phase]
    if first:
        m_ref[...] = jnp.full_like(m_ref, NEG)
        l_ref[...] = jnp.zeros_like(l_ref)
        acc_ref[...] = jnp.zeros_like(acc_ref)
    project(chunks, wk_ref, wvt_ref, k_ref, vt_ref, norm_ref)
    before = bounded_ref[0] == 1
    fits = jnp.max(norm_ref[...]) * jnp.max(qnorm_ref[...]) * 1.02 * SCALE * SCALE <= LIMIT * LIMIT
    bounded = jnp.logical_and(before, fits)
    count = count_ref[phase]

    @pl.when(bounded)
    def _():
        visit_bounded(items_ref, count, words_ref, qbd_ref, k_ref, vt_ref, l_ref, acc_ref, w_refs)

    @pl.when(jnp.logical_not(bounded))
    def _():
        @pl.when(before)
        def _():
            m_ref[...] = jnp.where(l_ref[...] > 0, 0.0, NEG)

        visit(items_ref, count, words_ref, qbd_ref, k_ref, vt_ref, m_ref, l_ref, acc_ref, s_refs, x_refs, w_refs, f_refs)

    if last:
        def emit(q, carry):
            tot = l_ref[q, :HEADS, :]
            for h in range(HEADS):
                a = slice(h * HEAD, (h + 1) * HEAD)
                out_ref[q, a, :] = (acc_ref[q, a, :] / tot[h : h + 1, :]).astype(BF16)
            top = jnp.where(bounded, jnp.floor(jnp.log2(tot)), m_ref[q, :HEADS, :])
            high = top.astype(BF16).astype(F32)
            low = (top - high).astype(BF16).astype(F32)
            base = jnp.where(bounded, 0.0, top)
            mass = tot * jnp.exp2(base - high - low)
            mass_high = mass.astype(BF16).astype(F32)
            parts = [high, low, mass_high, mass - mass_high]
            out_ref[q, BLK:, :] = jnp.concatenate(parts, axis=0).astype(BF16)
            return carry

        lax.fori_loop(0, DESTS, emit, 0, unroll=4)
    else:
        out_ref[0] = bounded.astype(jnp.int32)


def run_phase(phase, items, count, words, qbd, qnorm, wk, wvt, chunks, state):
    first, last = phase == 0, phase == 2
    blocks = sum(c.shape[0] for c in chunks) // BLK
    out_shape = (
        jax.ShapeDtypeStruct((DESTS + 1, 8, BLK), F32),
        jax.ShapeDtypeStruct((DESTS + 1, 8, BLK), F32),
        jax.ShapeDtypeStruct((DESTS + 1, BLK, BLK), F32),
        jax.ShapeDtypeStruct((DESTS, MSG, BLK), BF16) if last else jax.ShapeDtypeStruct((1,), jnp.int32),
    )
    if first:
        state = (jnp.ones((1,), jnp.int32),)
    ins = (items, count, state[-1], words, qbd, qnorm, wk, wvt, *chunks, *state[:-1])
    specs = [smem()] * 3 + [vmem()] * (len(ins) - 3)
    return pl.pallas_call(
        functools.partial(phase_kernel, phase, len(chunks)),
        out_shape=out_shape,
        in_specs=specs,
        out_specs=(vmem(), vmem(), vmem(), vmem() if last else smem()),
        input_output_aliases={} if first else {len(ins) - 3 + i: i for i in range(3)},
        scratch_shapes=[
            pltpu.VMEM((blocks, BLK, BLK), BF16),
            pltpu.VMEM((blocks, BLK, BLK), BF16),
            pltpu.VMEM((8, BLK), F32),
            pltpu.VMEM((2 * BLK, HEADS * BLK), F32),
            pltpu.VMEM((2 * BLK, HEADS * BLK), F32),
            pltpu.VMEM((8, BLK), F32),
            pltpu.VMEM((8, BLK), F32),
            pltpu.VMEM((2 * BLK, HEADS * BLK), BF16),
            pltpu.VMEM((2 * BLK, HEADS * BLK), BF16),
            pltpu.VMEM((8, BLK), F32),
            pltpu.VMEM((8, BLK), F32),
        ],
        compiler_params=pltpu.CompilerParams(vmem_limit_bytes=24 * 1024 * 1024),
        cost_estimate=pl.CostEstimate(flops=500_000_000, bytes_accessed=8_000_000, transcendentals=4_000_000),
    )(*ins)


def combine_kernel(msg_ref, wo_ref, out_ref):
    sources = msg_ref.shape[0]
    for b in range(2):
        stats = []
        for j in range(sources):
            st = msg_ref[j, b, BLK:, :].astype(F32)
            stats.append((st[0:4] + st[4:8], st[8:12] + st[12:16]))
        peak = functools.reduce(jnp.maximum, [s[0] for s in stats])
        mass = [tot * jnp.exp2(top - peak) for top, tot in stats]
        denom = functools.reduce(jnp.add, mass)
        rows = []
        for h in range(HEADS):
            a = slice(h * HEAD, (h + 1) * HEAD)
            num = functools.reduce(
                jnp.add,
                [msg_ref[j, b, a, :].astype(F32) * mass[j][h : h + 1, :] for j in range(sources)],
            )
            rows.append(num / denom[h : h + 1, :])
        att = jnp.concatenate(rows, axis=0).astype(BF16)
        mixed = lax.dot_general(att, wo_ref[...], TN, preferred_element_type=F32)
        out_ref[b * BLK : (b + 1) * BLK, :] = mixed.astype(BF16)


def make_items(lists, counts, my_dst):
    my_x = my_dst // 8
    owner = lists // 2
    dx = (owner // 8 - my_x) % 4
    chunk = jnp.where(dx == 1, 1, 0)
    pos = (chunk * 8 + owner % 8) * 2 + lists % 2
    phase = jnp.where(dx == 0, 0, jnp.where(dx == 2, 2, 1))
    slots = jnp.arange(SLOTS, dtype=jnp.int32)
    dests = jnp.arange(DESTS, dtype=jnp.int32)
    word = dests[:, None] * SLOTS + slots[None, :]
    live = slots[None, :] < counts[:, None]
    pay = word | (pos << 8) | (1 << 16)
    sel = live[None] & (phase[None] == jnp.arange(3, dtype=jnp.int32)[:, None, None])
    sel_i = sel.astype(jnp.int32)
    before = (slots[None, :] < slots[:, None]).astype(jnp.int32)
    rank = jnp.sum(sel_i[:, :, None, :] * before[None, None], axis=-1)
    per_dest = (jnp.sum(sel_i, axis=-1) + 1) // 2
    offset = jnp.sum(per_dest[:, None, :] * before[None], axis=-1)
    total = jnp.sum(per_dest, axis=-1)
    item = jnp.where(sel, offset[:, :, None] + rank // 2 + 2, -1)
    key = (item * 2 + rank % 2).reshape(3, 1, DESTS * SLOTS)
    want = jnp.arange(2 * ITEMS, dtype=jnp.int32)
    want = (want % ITEMS) * 2 + want // ITEMS
    table = jnp.sum(jnp.where(key == want[None, :, None], pay.reshape(1, 1, -1), 0), axis=-1)
    return table.reshape(3, 2, ITEMS), total


def x_step(rows, step):
    return lax.ppermute(rows, "dst", [(x * 8 + z, ((x + step) % 4) * 8 + z) for x in range(4) for z in range(8)])


def shards(node_feats, w_query, w_key, w_value, w_out, src_blocks, live_counts, edge_bits):
    own = node_feats[0, 0]
    columns = [[x * 8 + z for z in range(8)] for x in range(4)]
    copies = pl.pallas_call(
        copy_kernel,
        out_shape=jax.ShapeDtypeStruct((8, 2 * BLK, BLK), BF16),
        in_specs=[vmem()],
        out_specs=vmem(),
    )(own)
    base = lax.all_to_all(copies, "dst", 0, 0, axis_index_groups=columns, tiled=True)
    base = base.reshape(16 * BLK, BLK)
    sent, _ = lax.optimization_barrier((own, copies))
    dest_rows = [own] + [lax.ppermute(sent, "src", [(i, (i + s) % 8) for i in range(8)]) for s in range(1, 8)]
    items, total = make_items(src_blocks[0, 0], live_counts[0, 0], lax.axis_index("dst"))
    words = edge_bits[0, 0].reshape(DESTS * SLOTS, 16, BLK)
    qbd, wvt, qnorm = pl.pallas_call(
        prep_kernel,
        out_shape=(
            jax.ShapeDtypeStruct((DESTS, BLK, HEADS * BLK), BF16),
            jax.ShapeDtypeStruct((BLK, BLK), BF16),
            jax.ShapeDtypeStruct((HEADS, 2 * BLK), F32),
        ),
        in_specs=[smem()] + [vmem()] * 10,
        out_specs=(vmem(), vmem(), vmem()),
        compiler_params=pltpu.CompilerParams(vmem_limit_bytes=16 * 1024 * 1024),
    )(lax.axis_index("src").reshape(1), *dest_rows, w_query, w_value)
    base, qnorm, items, total = lax.optimization_barrier((base, qnorm, items, total))
    left = x_step(base, 1)
    right = x_step(base, -1)
    run = functools.partial(run_phase, words=words, qbd=qbd, qnorm=qnorm, wk=w_key, wvt=wvt)
    state = run(0, items, total, chunks=[base], state=None)
    late, left, right, *state = lax.optimization_barrier((base, left, right, *state))
    far = x_step(late, 2)
    state = run(1, items, total, chunks=[left, right], state=state)
    msg = run(2, items, total, chunks=[far], state=state)
    got = lax.all_to_all(msg[3].reshape(8, 2, MSG, BLK), "src", 0, 0, tiled=True)
    mixed = pl.pallas_call(
        combine_kernel,
        out_shape=jax.ShapeDtypeStruct((2 * BLK, BLK), BF16),
        in_specs=[vmem(), vmem()],
        out_specs=vmem(),
    )(got, w_out)
    return mixed.reshape(1, 1, 2 * BLK, BLK)


def solution(mesh):
    in_specs = (
        P("src", "dst", None, None),
        P(),
        P(),
        P(),
        P(),
        P("src", "dst", None, None),
        P("src", "dst", None),
        P("src", "dst", None, None, None, None),
    )
    out_specs = P("src", "dst", None, None)
    return jax.shard_map(shards, mesh=mesh, in_specs=in_specs, out_specs=out_specs, check_vma=False)
```

```python
import functools
import math

import jax
import jax.numpy as jnp
from jax import lax
from jax.experimental import pallas as pl
from jax.experimental.pallas import tpu as pltpu
from jax.sharding import PartitionSpec as P

HEADS = 4
BLK = 128
HEAD = 32
DESTS = 16
SLOTS = 16
ITEMS = 144
NEG = -1e30
MSG = 144
LIMIT = 100.0
SCALE = math.log2(math.e) / math.sqrt(HEAD)
BF16 = jnp.bfloat16
F32 = jnp.float32
NT = (((1,), (1,)), ((), ()))
TN = (((0,), (0,)), ((), ()))


def vmem():
    return pl.BlockSpec(memory_space=pltpu.VMEM)


def smem():
    return pl.BlockSpec(memory_space=pltpu.SMEM)


def copy_kernel(own_ref, out_ref):
    for i in range(8):
        out_ref[i] = own_ref[...]


def prepare(me, row_refs, wq_ref, wv_ref, qbd_ref, wvt_ref, qnorm_ref):
    qbd_ref[...] = jnp.zeros_like(qbd_ref)
    wvt_ref[...] = wv_ref[...].T
    wqt = wq_ref[...].T
    norm = jnp.zeros((HEADS, 2 * BLK), F32)
    for step in range(8):
        owner = (me - step) & 7
        qt = lax.dot_general(wqt, row_refs[step][...], NT, preferred_element_type=F32).astype(BF16)
        wide = qt.astype(F32)
        norm = jnp.maximum(norm, jnp.sum((wide * wide).reshape(HEADS, HEAD, 2 * BLK), axis=1))
        for k in range(2):
            for h in range(HEADS):
                r = slice(h * HEAD, (h + 1) * HEAD)
                qbd_ref[2 * owner + k, r, h * BLK : (h + 1) * BLK] = qt[r, k * BLK : (k + 1) * BLK]
    qnorm_ref[...] = norm


def project(chunk_refs, wk_ref, wvt_ref, k_ref, vt_ref, norm_ref):
    col = lax.shift_right_logical(lax.broadcasted_iota(jnp.int32, (BLK, BLK), 0), 5)
    row = lax.shift_right_logical(lax.broadcasted_iota(jnp.int32, (BLK, BLK), 1), 5)
    same = (col == row).astype(BF16)
    norm_ref[...] = jnp.zeros_like(norm_ref)
    for n, chunk_ref in enumerate(chunk_refs):
        per = chunk_ref.shape[0] // 512

        def body(i, carry, n=n, chunk_ref=chunk_ref, per=per):
            rows = chunk_ref[pl.ds(i * 512, 512), :]
            keys = jnp.dot(rows, wk_ref[...], preferred_element_type=F32).astype(BF16)
            vals = lax.dot_general(wvt_ref[...], rows, NT, preferred_element_type=F32).astype(BF16)
            wide = keys.astype(F32)
            norms = jnp.dot((wide * wide).astype(BF16), same, preferred_element_type=F32)
            norm_ref[...] = jnp.maximum(norm_ref[...], jnp.max(norms.reshape(64, 8, BLK), axis=0))
            at = (n * per + i) * 4
            for k in range(4):
                t = slice(k * BLK, (k + 1) * BLK)
                k_ref[at + k] = keys[t]
                vt_ref[at + k] = vals[:, t]
            return carry

        lax.fori_loop(0, per, body, 0, unroll=4)


def fields(items_ref, i):
    p1 = items_ref[0, i]
    p2 = items_ref[1, i]
    live1 = lax.shift_right_logical(p1, 16)
    live2 = lax.shift_right_logical(p2, 16)
    w1 = p1 & 255
    w2 = p2 & 255
    b1 = lax.shift_right_logical(p1, 8) & 255
    b2 = lax.shift_right_logical(p2, 8) & 255
    q = lax.shift_right_logical(w1, 4)
    return q, jnp.where(live1 == 1, q, DESTS), b1, b2, w1, w2, live1, live2


def bit_of_row():
    sub_iota = lax.broadcasted_iota(jnp.int32, (8, BLK), 0)
    return jnp.left_shift(jnp.ones((8, BLK), jnp.int32), sub_iota)


def visit_bounded(items_ref, count, words_ref, qbd_ref, k_ref, vt_ref, l_ref, acc_ref, w_refs):
    bit = bit_of_row()
    ones = jnp.ones((16, 2 * BLK), BF16)

    def values_dot(i, w_ref):
        _, qd, b1, b2, _, _, _, _ = fields(items_ref, i)
        out = []
        for p in range(2):
            r = slice(64 * p, 64 * p + 64)
            lhs = jnp.concatenate([vt_ref[b1, r, :], vt_ref[b2, r, :]], axis=1)
            lhs = jnp.concatenate([lhs, ones], axis=0)
            out.append(jnp.dot(lhs, w_ref[:, 256 * p : 256 * p + 256], preferred_element_type=F32))
        return qd, out

    def values_add(qd, out):
        for p in range(2):
            o = out[p]
            for k in range(2):
                h = 2 * p + k
                c = slice(BLK * k, BLK * k + BLK)
                a = slice(h * HEAD, (h + 1) * HEAD)
                acc_ref[qd, a, :] += o[k * HEAD : (k + 1) * HEAD, c]
                l_ref[qd, h : h + 1, :] += o[64:65, c]

    def score(i, p):
        q, _, b1, b2, _, _, _, _ = fields(items_ref, i)
        kk = jnp.concatenate([k_ref[b1], k_ref[b2]], axis=0)
        return jnp.dot(kk, qbd_ref[q, :, 256 * p : 256 * p + 256], preferred_element_type=F32)

    def weigh(i, p, s, w_ref):
        _, _, _, _, w1, w2, live1, live2 = fields(items_ref, i)
        words = [words_ref[w1] * live1, words_ref[w2] * live2]
        for g in range(16):
            hits = []
            for u in (2 * g, 2 * g + 1):
                line = words[u // 16][u % 16 : u % 16 + 1, :]
                hits.append((jnp.broadcast_to(line, (8, BLK)) & bit) != 0)
            for k in range(2):
                v = [
                    jnp.exp2(jnp.where(hits[u], s[16 * g + 8 * u : 16 * g + 8 * u + 8, BLK * k : BLK * k + BLK] * SCALE, NEG))
                    for u in range(2)
                ]
                c = slice(256 * p + BLK * k, 256 * p + BLK * k + BLK)
                w_ref[16 * g : 16 * g + 16, c] = jnp.concatenate(v, axis=0).astype(BF16)

    def body(j, carry):
        for e in range(4):
            i = 4 * j + e
            if e == 0:
                s = [score(i + 2, 0), score(i + 2, 1)]
            weigh(i + 2, 0, s[0], w_refs[e % 2])
            nxt = [score(i + 3, 0)] if e < 3 else []
            weigh(i + 2, 1, s[1], w_refs[e % 2])
            if e < 3:
                nxt.append(score(i + 3, 1))
            qd, o = values_dot(i + 1, w_refs[1 - e % 2])
            values_add(qd, o)
            s = nxt
        return carry

    lax.fori_loop(0, lax.shift_right_logical(count + 4, 2), body, 0)


def visit(items_ref, count, words_ref, qbd_ref, k_ref, vt_ref, m_ref, l_ref, acc_ref, s_refs, x_refs, w_refs, f_refs):
    bit = bit_of_row()
    ones = jnp.ones((16, 2 * BLK), BF16)

    def gather_values(i, w_ref, f_ref):
        _, qd, b1, b2, _, _, _, _ = fields(items_ref, i)
        for p in range(2):
            r = slice(64 * p, 64 * p + 64)
            lhs = jnp.concatenate([vt_ref[b1, r, :], vt_ref[b2, r, :]], axis=1)
            lhs = jnp.concatenate([lhs, ones], axis=0)
            o = jnp.dot(lhs, w_ref[:, 256 * p : 256 * p + 256], preferred_element_type=F32)
            for k in range(2):
                h = 2 * p + k
                c = slice(BLK * k, BLK * k + BLK)
                fac = f_ref[h : h + 1, :]
                a = slice(h * HEAD, (h + 1) * HEAD)
                acc_ref[qd, a, :] = acc_ref[qd, a, :] * fac + o[k * HEAD : (k + 1) * HEAD, c]
                l_ref[qd, h : h + 1, :] = l_ref[qd, h : h + 1, :] * fac + o[64:65, c]

    def weigh(i, s_ref, x_ref, w_ref, f_ref):
        _, qd, _, _, _, _, _, _ = fields(items_ref, i)
        for h in range(HEADS):
            c = slice(BLK * h, BLK * h + BLK)
            old = m_ref[qd, h : h + 1, :]
            new = jnp.maximum(old, x_ref[h : h + 1, :])
            f_ref[h : h + 1, :] = jnp.exp2(old - new)
            m_ref[qd, h : h + 1, :] = new
            w_ref[:, c] = jnp.exp2(s_ref[:, c] - new).astype(BF16)

    def score(i, s_ref, x_ref):
        q, _, b1, b2, w1, w2, live1, live2 = fields(items_ref, i)
        kk = jnp.concatenate([k_ref[b1], k_ref[b2]], axis=0)
        words = [words_ref[w1] * live1, words_ref[w2] * live2]
        for p in range(2):
            s = jnp.dot(kk, qbd_ref[q, :, 256 * p : 256 * p + 256], preferred_element_type=F32)
            peak = [None, None]
            for g in range(32):
                row = words[g // 16][g % 16 : g % 16 + 1, :]
                hit = (jnp.broadcast_to(row, (8, BLK)) & bit) != 0
                for k in range(2):
                    v = jnp.where(hit, s[8 * g : 8 * g + 8, BLK * k : BLK * k + BLK] * SCALE, NEG)
                    s_ref[8 * g : 8 * g + 8, 256 * p + BLK * k : 256 * p + BLK * k + BLK] = v
                    peak[k] = v if peak[k] is None else jnp.maximum(peak[k], v)
            for k in range(2):
                x_ref[2 * p + k : 2 * p + k + 1, :] = jnp.max(peak[k], axis=0, keepdims=True)

    def body(j, carry):
        for e in range(2):
            i = 2 * j + e
            score(i + 2, s_refs[e], x_refs[e])
            gather_values(i, w_refs[e], f_refs[e])
            weigh(i + 1, s_refs[1 - e], x_refs[1 - e], w_refs[1 - e], f_refs[1 - e])
        return carry

    lax.fori_loop(0, lax.shift_right_logical(count + 3, 1), body, 0)


def phase_kernel(phase, n_chunks, items_ref, count_ref, flag_ref, words_ref, wk_ref, *refs):
    first, last = phase == 0, phase == 2
    chunks, refs = refs[:n_chunks], refs[n_chunks:]
    if first:
        row_refs, (wq_ref, wv_ref), refs = refs[:8], refs[8:10], refs[10:]
        m_ref, l_ref, acc_ref, out_ref, qbd_ref, wvt_ref, qnorm_ref = refs[:7]
        refs = refs[7:]
        prepare(flag_ref[0], row_refs, wq_ref, wv_ref, qbd_ref, wvt_ref, qnorm_ref)
    else:
        qbd_ref, wvt_ref, qnorm_ref = refs[:3]
        m_ref, l_ref, acc_ref, out_ref = refs[6:10]
        refs = refs[10:]
    k_ref, vt_ref, norm_ref = refs[:3]
    s_refs, x_refs, w_refs, f_refs = refs[3:5], refs[5:7], refs[7:9], refs[9:11]
    items_ref = items_ref.at[phase]
    if first:
        m_ref[...] = jnp.full_like(m_ref, NEG)
        l_ref[...] = jnp.zeros_like(l_ref)
        acc_ref[...] = jnp.zeros_like(acc_ref)
    project(chunks, wk_ref, wvt_ref, k_ref, vt_ref, norm_ref)
    before = True if first else flag_ref[0] == 1
    fits = jnp.max(norm_ref[...]) * jnp.max(qnorm_ref[...]) * 1.02 * SCALE * SCALE <= LIMIT * LIMIT
    bounded = fits if first else jnp.logical_and(before, fits)
    count = count_ref[phase]

    @pl.when(bounded)
    def _():
        visit_bounded(items_ref, count, words_ref, qbd_ref, k_ref, vt_ref, l_ref, acc_ref, w_refs)

    @pl.when(jnp.logical_not(bounded))
    def _():
        @pl.when(before)
        def _():
            m_ref[...] = jnp.where(l_ref[...] > 0, 0.0, NEG)

        visit(items_ref, count, words_ref, qbd_ref, k_ref, vt_ref, m_ref, l_ref, acc_ref, s_refs, x_refs, w_refs, f_refs)

    if last:
        def emit(q, carry):
            to = 14 - (q | 1) + 1 + (q & 1)
            tot = l_ref[q, :HEADS, :]
            for h in range(HEADS):
                a = slice(h * HEAD, (h + 1) * HEAD)
                out_ref[to, a, :] = (acc_ref[q, a, :] / tot[h : h + 1, :]).astype(BF16)
            top = jnp.where(bounded, jnp.floor(jnp.log2(tot)), m_ref[q, :HEADS, :])
            high = top.astype(BF16).astype(F32)
            low = (top - high).astype(BF16).astype(F32)
            base = jnp.where(bounded, 0.0, top)
            mass = tot * jnp.exp2(base - high - low)
            mass_high = mass.astype(BF16).astype(F32)
            parts = [high, low, mass_high, mass - mass_high]
            out_ref[to, BLK:, :] = jnp.concatenate(parts, axis=0).astype(BF16)
            return carry

        lax.fori_loop(0, DESTS, emit, 0, unroll=4)
    else:
        out_ref[0] = bounded.astype(jnp.int32)


def run_phase(phase, items, total, flag, words, wk, chunks, fixed=None, state=None, rows=None, weights=None):
    first, last = phase == 0, phase == 2
    blocks = sum(c.shape[0] for c in chunks) // BLK
    out_shape = [
        jax.ShapeDtypeStruct((DESTS + 1, 8, BLK), F32),
        jax.ShapeDtypeStruct((DESTS + 1, 8, BLK), F32),
        jax.ShapeDtypeStruct((DESTS + 1, BLK, BLK), F32),
        jax.ShapeDtypeStruct((DESTS, MSG, BLK), BF16) if last else jax.ShapeDtypeStruct((1,), jnp.int32),
    ]
    out_specs = [vmem(), vmem(), vmem(), vmem() if last else smem()]
    if first:
        out_shape += [
            jax.ShapeDtypeStruct((DESTS, BLK, HEADS * BLK), BF16),
            jax.ShapeDtypeStruct((BLK, BLK), BF16),
            jax.ShapeDtypeStruct((HEADS, 2 * BLK), F32),
        ]
        out_specs += [vmem()] * 3
    tail = (*rows, *weights) if first else (*fixed, *state)
    ins = (items, total, flag, words, wk, *chunks, *tail)
    return pl.pallas_call(
        functools.partial(phase_kernel, phase, len(chunks)),
        out_shape=out_shape,
        in_specs=[smem()] * 3 + [vmem()] * (len(ins) - 3),
        out_specs=out_specs,
        input_output_aliases={} if first else {len(ins) - 3 + i: i for i in range(3)},
        scratch_shapes=[
            pltpu.VMEM((blocks, BLK, BLK), BF16),
            pltpu.VMEM((blocks, BLK, BLK), BF16),
            pltpu.VMEM((8, BLK), F32),
            pltpu.VMEM((2 * BLK, HEADS * BLK), F32),
            pltpu.VMEM((2 * BLK, HEADS * BLK), F32),
            pltpu.VMEM((8, BLK), F32),
            pltpu.VMEM((8, BLK), F32),
            pltpu.VMEM((2 * BLK, HEADS * BLK), BF16),
            pltpu.VMEM((2 * BLK, HEADS * BLK), BF16),
            pltpu.VMEM((8, BLK), F32),
            pltpu.VMEM((8, BLK), F32),
        ],
        compiler_params=pltpu.CompilerParams(vmem_limit_bytes=10 * 1024 * 1024),
        cost_estimate=pl.CostEstimate(flops=500_000_000, bytes_accessed=8_000_000, transcendentals=4_000_000),
    )(*ins)


def combine_kernel(msg_ref, wo_ref, out_ref):
    sources = msg_ref.shape[0]
    for b in range(2):
        stats = []
        for j in range(sources):
            st = msg_ref[j, b, BLK:, :].astype(F32)
            stats.append((st[0:4] + st[4:8], st[8:12] + st[12:16]))
        peak = functools.reduce(jnp.maximum, [s[0] for s in stats])
        mass = [tot * jnp.exp2(top - peak) for top, tot in stats]
        denom = functools.reduce(jnp.add, mass)
        rows = []
        for h in range(HEADS):
            a = slice(h * HEAD, (h + 1) * HEAD)
            num = functools.reduce(
                jnp.add,
                [msg_ref[j, b, a, :].astype(F32) * mass[j][h : h + 1, :] for j in range(sources)],
            )
            rows.append(num / denom[h : h + 1, :])
        att = jnp.concatenate(rows, axis=0).astype(BF16)
        mixed = lax.dot_general(att, wo_ref[...], TN, preferred_element_type=F32)
        out_ref[b * BLK : (b + 1) * BLK, :] = mixed.astype(BF16)


def make_items(lists, counts, my_dst):
    my_x = my_dst // 8
    owner = lists // 2
    dx = (owner // 8 - my_x) % 4
    chunk = jnp.where(dx == 1, 1, 0)
    pos = (chunk * 8 + 7 - owner % 8) * 2 + lists % 2
    phase = jnp.where(dx == 0, 0, jnp.where(dx == 2, 2, 1))
    slots = jnp.arange(SLOTS, dtype=jnp.int32)
    dests = jnp.arange(DESTS, dtype=jnp.int32)
    word = dests[:, None] * SLOTS + slots[None, :]
    live = slots[None, :] < counts[:, None]
    pay = word | (pos << 8) | (1 << 16)
    sel = live[None] & (phase[None] == jnp.arange(3, dtype=jnp.int32)[:, None, None])
    sel_i = sel.astype(jnp.int32)
    before = (slots[None, :] < slots[:, None]).astype(jnp.int32)
    rank = jnp.sum(sel_i[:, :, None, :] * before[None, None], axis=-1)
    per_dest = (jnp.sum(sel_i, axis=-1) + 1) // 2
    offset = jnp.sum(per_dest[:, None, :] * before[None], axis=-1)
    total = jnp.sum(per_dest, axis=-1)
    item = jnp.where(sel, offset[:, :, None] + rank // 2 + 2, -1)
    key = (item * 2 + rank % 2).reshape(3, 1, DESTS * SLOTS)
    want = jnp.arange(2 * ITEMS, dtype=jnp.int32)
    want = (want % ITEMS) * 2 + want // ITEMS
    table = jnp.sum(jnp.where(key == want[None, :, None], pay.reshape(1, 1, -1), 0), axis=-1)
    return table.reshape(3, 2, ITEMS), total


def x_step(rows, step):
    return lax.ppermute(rows, "dst", [(x * 8 + z, ((x + step) % 4) * 8 + z) for x in range(4) for z in range(8)])


def shards(node_feats, w_query, w_key, w_value, w_out, src_blocks, live_counts, edge_bits):
    own = node_feats[0, 0]
    columns = [[x * 8 + 7 - z for z in range(8)] for x in range(4)]
    copies = pl.pallas_call(
        copy_kernel,
        out_shape=jax.ShapeDtypeStruct((8, 2 * BLK, BLK), BF16),
        in_specs=[vmem()],
        out_specs=vmem(),
    )(own)
    base = lax.all_to_all(copies, "dst", 0, 0, axis_index_groups=columns, tiled=True)
    base = base.reshape(16 * BLK, BLK)
    sent, _ = lax.optimization_barrier((own, copies))
    dest_rows = [own] + [lax.ppermute(sent, "src", [(i, (i + s) % 8) for i in range(8)]) for s in range(1, 8)]
    items, total = make_items(src_blocks[0, 0], live_counts[0, 0], lax.axis_index("dst"))
    words = edge_bits[0, 0].reshape(DESTS * SLOTS, 16, BLK)
    base, items, total, *others = lax.optimization_barrier((base, items, total, *dest_rows[1:]))
    left = x_step(base, 1)
    right = x_step(base, -1)
    run = functools.partial(run_phase, items=items, total=total, words=words, wk=w_key)
    out = run(0, flag=lax.axis_index("src").reshape(1), chunks=[base], rows=[own, *others], weights=(w_query, w_value))
    state, flag, fixed = out[:3], out[3], out[4:]
    late, left, right, flag = lax.optimization_barrier((base, left, right, flag))
    far = x_step(late, 2)
    *state, flag = run(1, flag=flag, chunks=[left, right], fixed=fixed, state=state)
    msg = run(2, flag=flag, chunks=[far], fixed=fixed, state=state)
    got = lax.all_to_all(
        msg[3].reshape(8, 2, MSG, BLK), "src", 0, 0, axis_index_groups=[list(range(7, -1, -1))], tiled=True
    )
    mixed = pl.pallas_call(
        combine_kernel,
        out_shape=jax.ShapeDtypeStruct((2 * BLK, BLK), BF16),
        in_specs=[vmem(), vmem()],
        out_specs=vmem(),
    )(got, w_out)
    return mixed.reshape(1, 1, 2 * BLK, BLK)


def solution(mesh):
    in_specs = (
        P("src", "dst", None, None),
        P(),
        P(),
        P(),
        P(),
        P("src", "dst", None, None),
        P("src", "dst", None),
        P("src", "dst", None, None, None, None),
    )
    out_specs = P("src", "dst", None, None)
    return jax.shard_map(shards, mesh=mesh, in_specs=in_specs, out_specs=out_specs, check_vma=False)
```

```python
import functools
import math

import jax
import jax.numpy as jnp
from jax import lax
from jax.experimental import pallas as pl
from jax.experimental.pallas import tpu as pltpu
from jax.sharding import PartitionSpec as P

HEADS = 4
BLK = 128
HEAD = 32
DESTS = 16
SLOTS = 16
ITEMS = 144
NEG = -1e30
MSG = 144
LIMIT = 100.0
SCALE = math.log2(math.e) / math.sqrt(HEAD)
BF16 = jnp.bfloat16
F32 = jnp.float32
NT = (((1,), (1,)), ((), ()))
TN = (((0,), (0,)), ((), ()))


def vmem():
    return pl.BlockSpec(memory_space=pltpu.VMEM)


def smem():
    return pl.BlockSpec(memory_space=pltpu.SMEM)


def copy_kernel(own_ref, out_ref):
    for i in range(8):
        out_ref[i] = own_ref[...]


def prepare(me, row_refs, wq_ref, wv_ref, qbd_ref, wvt_ref, qnorm_ref):
    qbd_ref[...] = jnp.zeros_like(qbd_ref)
    wvt_ref[...] = wv_ref[...].T
    wqt = wq_ref[...].T
    norm = jnp.zeros((HEADS, 2 * BLK), F32)
    for step in range(8):
        owner = (me - step) & 7
        qt = lax.dot_general(wqt, row_refs[step][...], NT, preferred_element_type=F32).astype(BF16)
        wide = qt.astype(F32)
        norm = jnp.maximum(norm, jnp.sum((wide * wide).reshape(HEADS, HEAD, 2 * BLK), axis=1))
        for k in range(2):
            for h in range(HEADS):
                r = slice(h * HEAD, (h + 1) * HEAD)
                qbd_ref[2 * owner + k, r, h * BLK : (h + 1) * BLK] = qt[r, k * BLK : (k + 1) * BLK]
    qnorm_ref[...] = norm


def project(chunk_refs, wk_ref, wvt_ref, k_ref, vt_ref, norm_ref):
    col = lax.shift_right_logical(lax.broadcasted_iota(jnp.int32, (BLK, BLK), 0), 5)
    row = lax.shift_right_logical(lax.broadcasted_iota(jnp.int32, (BLK, BLK), 1), 5)
    same = (col == row).astype(BF16)
    norm_ref[...] = jnp.zeros_like(norm_ref)
    for n, chunk_ref in enumerate(chunk_refs):
        per = chunk_ref.shape[0] // 512

        def body(i, carry, n=n, chunk_ref=chunk_ref, per=per):
            rows = chunk_ref[pl.ds(i * 512, 512), :]
            keys = jnp.dot(rows, wk_ref[...], preferred_element_type=F32).astype(BF16)
            vals = lax.dot_general(wvt_ref[...], rows, NT, preferred_element_type=F32).astype(BF16)
            wide = keys.astype(F32)
            norms = jnp.dot((wide * wide).astype(BF16), same, preferred_element_type=F32)
            norm_ref[...] = jnp.maximum(norm_ref[...], jnp.max(norms.reshape(64, 8, BLK), axis=0))
            at = (n * per + i) * 4
            for k in range(4):
                t = slice(k * BLK, (k + 1) * BLK)
                k_ref[at + k] = keys[t]
                vt_ref[at + k] = vals[:, t]
            return carry

        lax.fori_loop(0, per, body, 0, unroll=4)


def fields(items_ref, i):
    p1 = items_ref[0, i]
    p2 = items_ref[1, i]
    live1 = lax.shift_right_logical(p1, 16)
    live2 = lax.shift_right_logical(p2, 16)
    w1 = p1 & 255
    w2 = p2 & 255
    b1 = lax.shift_right_logical(p1, 8) & 255
    b2 = lax.shift_right_logical(p2, 8) & 255
    q = lax.shift_right_logical(w1, 4)
    return q, jnp.where(live1 == 1, q, DESTS), b1, b2, w1, w2, live1, live2


def bit_of_row():
    sub_iota = lax.broadcasted_iota(jnp.int32, (8, BLK), 0)
    return jnp.left_shift(jnp.ones((8, BLK), jnp.int32), sub_iota)


def visit_bounded(items_ref, count, words_ref, qbd_ref, k_ref, vt_ref, l_ref, acc_ref, w_refs):
    bit = bit_of_row()
    ones = jnp.ones((16, 2 * BLK), BF16)

    def values_dot(i, w_ref):
        _, qd, b1, b2, _, _, _, _ = fields(items_ref, i)
        out = []
        for p in range(2):
            r = slice(64 * p, 64 * p + 64)
            lhs = jnp.concatenate([vt_ref[b1, r, :], vt_ref[b2, r, :]], axis=1)
            lhs = jnp.concatenate([lhs, ones], axis=0)
            out.append(jnp.dot(lhs, w_ref[:, 256 * p : 256 * p + 256], preferred_element_type=F32))
        return qd, out

    def values_add(qd, out):
        for p in range(2):
            o = out[p]
            for k in range(2):
                h = 2 * p + k
                c = slice(BLK * k, BLK * k + BLK)
                a = slice(h * HEAD, (h + 1) * HEAD)
                acc_ref[qd, a, :] += o[k * HEAD : (k + 1) * HEAD, c]
                l_ref[qd, h : h + 1, :] += o[64:65, c]

    def score(i, p):
        q, _, b1, b2, _, _, _, _ = fields(items_ref, i)
        kk = jnp.concatenate([k_ref[b1], k_ref[b2]], axis=0)
        return jnp.dot(kk, qbd_ref[q, :, 256 * p : 256 * p + 256], preferred_element_type=F32)

    def weigh(i, p, s, w_ref):
        _, _, _, _, w1, w2, live1, live2 = fields(items_ref, i)
        words = [words_ref[w1] * live1, words_ref[w2] * live2]
        for g in range(16):
            hits = []
            for u in (2 * g, 2 * g + 1):
                line = words[u // 16][u % 16 : u % 16 + 1, :]
                hits.append((jnp.broadcast_to(line, (8, BLK)) & bit) != 0)
            for k in range(2):
                v = [
                    jnp.exp2(jnp.where(hits[u], s[16 * g + 8 * u : 16 * g + 8 * u + 8, BLK * k : BLK * k + BLK] * SCALE, NEG))
                    for u in range(2)
                ]
                c = slice(256 * p + BLK * k, 256 * p + BLK * k + BLK)
                w_ref[16 * g : 16 * g + 16, c] = jnp.concatenate(v, axis=0).astype(BF16)

    def body(j, carry):
        for e in range(4):
            i = 4 * j + e
            if e == 0:
                s = [score(i + 2, 0), score(i + 2, 1)]
            weigh(i + 2, 0, s[0], w_refs[e % 2])
            nxt = [score(i + 3, 0)] if e < 3 else []
            weigh(i + 2, 1, s[1], w_refs[e % 2])
            if e < 3:
                nxt.append(score(i + 3, 1))
            qd, o = values_dot(i + 1, w_refs[1 - e % 2])
            values_add(qd, o)
            s = nxt
        return carry

    lax.fori_loop(0, lax.shift_right_logical(count + 4, 2), body, 0)


def visit(items_ref, count, words_ref, qbd_ref, k_ref, vt_ref, m_ref, l_ref, acc_ref, s_refs, x_refs, w_refs, f_refs):
    bit = bit_of_row()
    ones = jnp.ones((16, 2 * BLK), BF16)

    def gather_values(i, w_ref, f_ref):
        _, qd, b1, b2, _, _, _, _ = fields(items_ref, i)
        for p in range(2):
            r = slice(64 * p, 64 * p + 64)
            lhs = jnp.concatenate([vt_ref[b1, r, :], vt_ref[b2, r, :]], axis=1)
            lhs = jnp.concatenate([lhs, ones], axis=0)
            o = jnp.dot(lhs, w_ref[:, 256 * p : 256 * p + 256], preferred_element_type=F32)
            for k in range(2):
                h = 2 * p + k
                c = slice(BLK * k, BLK * k + BLK)
                fac = f_ref[h : h + 1, :]
                a = slice(h * HEAD, (h + 1) * HEAD)
                acc_ref[qd, a, :] = acc_ref[qd, a, :] * fac + o[k * HEAD : (k + 1) * HEAD, c]
                l_ref[qd, h : h + 1, :] = l_ref[qd, h : h + 1, :] * fac + o[64:65, c]

    def weigh(i, s_ref, x_ref, w_ref, f_ref):
        _, qd, _, _, _, _, _, _ = fields(items_ref, i)
        for h in range(HEADS):
            c = slice(BLK * h, BLK * h + BLK)
            old = m_ref[qd, h : h + 1, :]
            new = jnp.maximum(old, x_ref[h : h + 1, :])
            f_ref[h : h + 1, :] = jnp.exp2(old - new)
            m_ref[qd, h : h + 1, :] = new
            w_ref[:, c] = jnp.exp2(s_ref[:, c] - new).astype(BF16)

    def score(i, s_ref, x_ref):
        q, _, b1, b2, w1, w2, live1, live2 = fields(items_ref, i)
        kk = jnp.concatenate([k_ref[b1], k_ref[b2]], axis=0)
        words = [words_ref[w1] * live1, words_ref[w2] * live2]
        for p in range(2):
            s = jnp.dot(kk, qbd_ref[q, :, 256 * p : 256 * p + 256], preferred_element_type=F32)
            peak = [None, None]
            for g in range(32):
                row = words[g // 16][g % 16 : g % 16 + 1, :]
                hit = (jnp.broadcast_to(row, (8, BLK)) & bit) != 0
                for k in range(2):
                    v = jnp.where(hit, s[8 * g : 8 * g + 8, BLK * k : BLK * k + BLK] * SCALE, NEG)
                    s_ref[8 * g : 8 * g + 8, 256 * p + BLK * k : 256 * p + BLK * k + BLK] = v
                    peak[k] = v if peak[k] is None else jnp.maximum(peak[k], v)
            for k in range(2):
                x_ref[2 * p + k : 2 * p + k + 1, :] = jnp.max(peak[k], axis=0, keepdims=True)

    def body(j, carry):
        for e in range(2):
            i = 2 * j + e
            score(i + 2, s_refs[e], x_refs[e])
            gather_values(i, w_refs[e], f_refs[e])
            weigh(i + 1, s_refs[1 - e], x_refs[1 - e], w_refs[1 - e], f_refs[1 - e])
        return carry

    lax.fori_loop(0, lax.shift_right_logical(count + 3, 1), body, 0)


def phase_kernel(phase, n_chunks, items_ref, count_ref, flag_ref, words_ref, wk_ref, *refs):
    first, last = phase == 0, phase == 2
    chunks, refs = refs[:n_chunks], refs[n_chunks:]
    if first:
        row_refs, (wq_ref, wv_ref), refs = refs[:8], refs[8:10], refs[10:]
        m_ref, l_ref, acc_ref, out_ref, qbd_ref, wvt_ref, qnorm_ref = refs[:7]
        refs = refs[7:]
        prepare(flag_ref[0], row_refs, wq_ref, wv_ref, qbd_ref, wvt_ref, qnorm_ref)
    else:
        qbd_ref, wvt_ref, qnorm_ref = refs[:3]
        m_ref, l_ref, acc_ref, out_ref = refs[6:10]
        refs = refs[10:]
    k_ref, vt_ref, norm_ref = refs[:3]
    s_refs, x_refs, w_refs, f_refs = refs[3:5], refs[5:7], refs[7:9], refs[9:11]
    items_ref = items_ref.at[phase]
    if first:
        m_ref[...] = jnp.full_like(m_ref, NEG)
        l_ref[...] = jnp.zeros_like(l_ref)
        acc_ref[...] = jnp.zeros_like(acc_ref)
    project(chunks, wk_ref, wvt_ref, k_ref, vt_ref, norm_ref)
    before = True if first else flag_ref[0] == 1
    fits = jnp.max(norm_ref[...]) * jnp.max(qnorm_ref[...]) * 1.02 * SCALE * SCALE <= LIMIT * LIMIT
    bounded = fits if first else jnp.logical_and(before, fits)
    count = count_ref[phase]

    @pl.when(bounded)
    def _():
        visit_bounded(items_ref, count, words_ref, qbd_ref, k_ref, vt_ref, l_ref, acc_ref, w_refs)

    @pl.when(jnp.logical_not(bounded))
    def _():
        @pl.when(before)
        def _():
            m_ref[...] = jnp.where(l_ref[...] > 0, 0.0, NEG)

        visit(items_ref, count, words_ref, qbd_ref, k_ref, vt_ref, m_ref, l_ref, acc_ref, s_refs, x_refs, w_refs, f_refs)

    if last:
        def emit(q, carry):
            to = 14 - (q | 1) + 1 + (q & 1)
            tot = l_ref[q, :HEADS, :]
            for h in range(HEADS):
                a = slice(h * HEAD, (h + 1) * HEAD)
                out_ref[to, a, :] = (acc_ref[q, a, :] / tot[h : h + 1, :]).astype(BF16)
            top = jnp.where(bounded, jnp.floor(jnp.log2(tot)), m_ref[q, :HEADS, :])
            high = top.astype(BF16).astype(F32)
            low = (top - high).astype(BF16).astype(F32)
            base = jnp.where(bounded, 0.0, top)
            mass = tot * jnp.exp2(base - high - low)
            mass_high = mass.astype(BF16).astype(F32)
            parts = [high, low, mass_high, mass - mass_high]
            out_ref[to, BLK:, :] = jnp.concatenate(parts, axis=0).astype(BF16)
            return carry

        lax.fori_loop(0, DESTS, emit, 0, unroll=4)
    else:
        out_ref[0] = bounded.astype(jnp.int32)


def run_phase(phase, items, total, flag, words, wk, chunks, fixed=None, state=None, rows=None, weights=None):
    first, last = phase == 0, phase == 2
    blocks = sum(c.shape[0] for c in chunks) // BLK
    out_shape = [
        jax.ShapeDtypeStruct((DESTS + 1, 8, BLK), F32),
        jax.ShapeDtypeStruct((DESTS + 1, 8, BLK), F32),
        jax.ShapeDtypeStruct((DESTS + 1, BLK, BLK), F32),
        jax.ShapeDtypeStruct((DESTS, MSG, BLK), BF16) if last else jax.ShapeDtypeStruct((1,), jnp.int32),
    ]
    out_specs = [vmem(), vmem(), vmem(), vmem() if last else smem()]
    if first:
        out_shape += [
            jax.ShapeDtypeStruct((DESTS, BLK, HEADS * BLK), BF16),
            jax.ShapeDtypeStruct((BLK, BLK), BF16),
            jax.ShapeDtypeStruct((HEADS, 2 * BLK), F32),
        ]
        out_specs += [vmem()] * 3
    tail = (*rows, *weights) if first else (*fixed, *state)
    ins = (items, total, flag, words, wk, *chunks, *tail)
    return pl.pallas_call(
        functools.partial(phase_kernel, phase, len(chunks)),
        out_shape=out_shape,
        in_specs=[smem()] * 3 + [vmem()] * (len(ins) - 3),
        out_specs=out_specs,
        input_output_aliases={} if first else {len(ins) - 3 + i: i for i in range(3)},
        scratch_shapes=[
            pltpu.VMEM((blocks, BLK, BLK), BF16),
            pltpu.VMEM((blocks, BLK, BLK), BF16),
            pltpu.VMEM((8, BLK), F32),
            pltpu.VMEM((2 * BLK, HEADS * BLK), F32),
            pltpu.VMEM((2 * BLK, HEADS * BLK), F32),
            pltpu.VMEM((8, BLK), F32),
            pltpu.VMEM((8, BLK), F32),
            pltpu.VMEM((2 * BLK, HEADS * BLK), BF16),
            pltpu.VMEM((2 * BLK, HEADS * BLK), BF16),
            pltpu.VMEM((8, BLK), F32),
            pltpu.VMEM((8, BLK), F32),
        ],
        compiler_params=pltpu.CompilerParams(vmem_limit_bytes=10 * 1024 * 1024),
        cost_estimate=pl.CostEstimate(flops=500_000_000, bytes_accessed=8_000_000, transcendentals=4_000_000),
    )(*ins)


def combine_kernel(msg_ref, wo_ref, out_ref):
    sources = msg_ref.shape[0]
    for b in range(2):
        stats = []
        for j in range(sources):
            st = msg_ref[j, b, BLK:, :].astype(F32)
            stats.append((st[0:4] + st[4:8], st[8:12] + st[12:16]))
        peak = functools.reduce(jnp.maximum, [s[0] for s in stats])
        mass = [tot * jnp.exp2(top - peak) for top, tot in stats]
        denom = functools.reduce(jnp.add, mass)
        rows = []
        for h in range(HEADS):
            a = slice(h * HEAD, (h + 1) * HEAD)
            num = functools.reduce(
                jnp.add,
                [msg_ref[j, b, a, :].astype(F32) * mass[j][h : h + 1, :] for j in range(sources)],
            )
            rows.append(num / denom[h : h + 1, :])
        att = jnp.concatenate(rows, axis=0).astype(BF16)
        mixed = lax.dot_general(att, wo_ref[...], TN, preferred_element_type=F32)
        out_ref[b * BLK : (b + 1) * BLK, :] = mixed.astype(BF16)


def make_items(lists, counts, my_dst):
    my_x = my_dst // 8
    owner = lists // 2
    dx = (owner // 8 - my_x) % 4
    chunk = jnp.where(dx == 1, 1, 0)
    z = owner % 8
    pos = (chunk * 8 + jnp.where(z < 6, z + 2, 7 - z)) * 2 + lists % 2
    phase = jnp.where(dx == 0, 0, jnp.where(dx == 2, 2, 1))
    slots = jnp.arange(SLOTS, dtype=jnp.int32)
    dests = jnp.arange(DESTS, dtype=jnp.int32)
    word = dests[:, None] * SLOTS + slots[None, :]
    live = slots[None, :] < counts[:, None]
    pay = word | (pos << 8) | (1 << 16)
    sel = live[None] & (phase[None] == jnp.arange(3, dtype=jnp.int32)[:, None, None])
    sel_i = sel.astype(jnp.int32)
    before = (slots[None, :] < slots[:, None]).astype(jnp.int32)
    rank = jnp.sum(sel_i[:, :, None, :] * before[None, None], axis=-1)
    per_dest = (jnp.sum(sel_i, axis=-1) + 1) // 2
    offset = jnp.sum(per_dest[:, None, :] * before[None], axis=-1)
    total = jnp.sum(per_dest, axis=-1)
    item = jnp.where(sel, offset[:, :, None] + rank // 2 + 2, -1)
    key = (item * 2 + rank % 2).reshape(3, 1, DESTS * SLOTS)
    want = jnp.arange(2 * ITEMS, dtype=jnp.int32)
    want = (want % ITEMS) * 2 + want // ITEMS
    table = jnp.sum(jnp.where(key == want[None, :, None], pay.reshape(1, 1, -1), 0), axis=-1)
    return table.reshape(3, 2, ITEMS), total


def x_step(rows, step):
    return lax.ppermute(rows, "dst", [(x * 8 + z, ((x + step) % 4) * 8 + z) for x in range(4) for z in range(8)])


def shards(node_feats, w_query, w_key, w_value, w_out, src_blocks, live_counts, edge_bits):
    own = node_feats[0, 0]
    columns = [[x * 8 + z for z in (7, 6, 0, 1, 2, 3, 4, 5)] for x in range(4)]
    copies = pl.pallas_call(
        copy_kernel,
        out_shape=jax.ShapeDtypeStruct((8, 2 * BLK, BLK), BF16),
        in_specs=[vmem()],
        out_specs=vmem(),
    )(own)
    base = lax.all_to_all(copies, "dst", 0, 0, axis_index_groups=columns, tiled=True)
    base = base.reshape(16 * BLK, BLK)
    sent, _ = lax.optimization_barrier((own, copies))
    dest_rows = [own] + [lax.ppermute(sent, "src", [(i, (i + s) % 8) for i in range(8)]) for s in range(1, 8)]
    items, total = make_items(src_blocks[0, 0], live_counts[0, 0], lax.axis_index("dst"))
    words = edge_bits[0, 0].reshape(DESTS * SLOTS, 16, BLK)
    base, items, total, *others = lax.optimization_barrier((base, items, total, *dest_rows[1:]))
    left = x_step(base, 1)
    right = x_step(base, -1)
    run = functools.partial(run_phase, items=items, total=total, words=words, wk=w_key)
    out = run(0, flag=lax.axis_index("src").reshape(1), chunks=[base], rows=[own, *others], weights=(w_query, w_value))
    state, flag, fixed = out[:3], out[3], out[4:]
    late, left, right, flag = lax.optimization_barrier((base, left, right, flag))
    far = x_step(late, 2)
    *state, flag = run(1, flag=flag, chunks=[left, right], fixed=fixed, state=state)
    msg = run(2, flag=flag, chunks=[far], fixed=fixed, state=state)
    got = lax.all_to_all(
        msg[3].reshape(8, 2, MSG, BLK), "src", 0, 0, axis_index_groups=[list(range(7, -1, -1))], tiled=True
    )
    mixed = pl.pallas_call(
        combine_kernel,
        out_shape=jax.ShapeDtypeStruct((2 * BLK, BLK), BF16),
        in_specs=[vmem(), vmem()],
        out_specs=vmem(),
    )(got, w_out)
    return mixed.reshape(1, 1, 2 * BLK, BLK)


def solution(mesh):
    in_specs = (
        P("src", "dst", None, None),
        P(),
        P(),
        P(),
        P(),
        P("src", "dst", None, None),
        P("src", "dst", None),
        P("src", "dst", None, None, None, None),
    )
    out_specs = P("src", "dst", None, None)
    return jax.shard_map(shards, mesh=mesh, in_specs=in_specs, out_specs=out_specs, check_vma=False)
```
